256 devices in a mesh: dom: 32 (over z, y_lo, core), tile: 8 (over y_hi, x).
Axes of the slice: x: 4, y: 4 (y_hi: 2, y_lo: 2; y = y_hi * 2 + y_lo), z: 8, core: 2. Of those that a mesh axis runs over, the one named last changes fastest.
Arguments:
- state: float32 [64, 3, 256, 1024], P('dom', None, 'tile'), may hold values from -6 to 6
- noise: float32 [64, 256, 1024], P('dom', 'tile'), may hold values from -4 to 4
- parents: int32 [64], replicated, may hold values from 0 to 63, as said below
- measured_cell_position: int32 [16384], P('tile'), may hold values from 0 to 262143, as said below
- obs_value: float32 [16384], P('tile'), may hold values from -6 to 6
- obs_precision: float32 [16384], P('tile'), may hold values from 0.3 to 27
Outputs:
- predicted_fields: float32 [64, 3, 256, 1024], P('dom', None, 'tile')
- observation_mismatch: float32 [64], P('dom')
The draws below stay inside these ranges and needn't reach their ends.
Inputs may be any that keep to these rules, and one draw needn't show every extreme that they name: parents never fall from one new particle to the next; the first is 0 and the last is 63. `measured_cell_position`: entries b * 2048 to (b + 1) * 2048 - 1 lie in rows b * 32 to (b + 1) * 32 - 1, all distinct; the first and last cell of those rows are observed.
All inputs are finite; a program needn't handle non-finite values.
Results may differ from the reference program's by a relative error of at most 0.00002.
Values sent between devices are 32-bit elements; how exact they have to be, the bound alone decides.
A program may use at most 128 MiB of HBM per device.

```python
import jax
import jax.numpy as jnp
from jax import lax

COLS = 1024
STEPS = 4
OBS_DEV = 2048
PARTICLES = 64
NY = 256
OBS = 16384


def draw_parents(key, part):
    key = jax.random.fold_in(key, 5)
    first, second = jax.random.split(key)
    left = jax.random.randint(first, (PARTICLES,), 0, PARTICLES)
    right = jax.random.randint(second, (PARTICLES,), 0, PARTICLES)
    picked = jnp.sort(jnp.minimum(left, right))
    picked = picked.at[0].set(0).at[PARTICLES - 1].set(PARTICLES - 1)
    return picked.astype(jnp.int32)


def draw_measured_cell_position(key, part):
    key = jax.random.fold_in(key, 3)
    strips = OBS // OBS_DEV
    cells = NY * COLS // strips
    keys = jax.random.split(key, strips)

    def one_strip(strip_key):
        order = jax.random.permutation(strip_key, cells - 2) + 1
        ends = jnp.array([0, cells - 1], jnp.int32)
        return jnp.concatenate([ends, order[:OBS_DEV - 2].astype(jnp.int32)])
    picks = jax.vmap(one_strip)(keys)
    strip_offsets = (jnp.arange(strips, dtype=jnp.int32) * cells)[:, None]
    return (picks + strip_offsets).reshape(-1).astype(jnp.int32)


def draw_obs_precision(key, part):
    key = jax.random.fold_in(key, 7)
    strips = OBS // OBS_DEV
    place = (jnp.arange(OBS) // OBS_DEV).astype(jnp.float32) / max(strips - 1, 1)
    base = jnp.exp(jax.random.uniform(key, (OBS,), jnp.float32, jnp.log(0.5), jnp.log(2.0)))
    rise = jnp.exp(place * jnp.log(3.0))
    return (base * rise).astype(jnp.float32)


def level_of(own_key, dims, shards, least, top_value):
    level = 1.0
    for axis_at, shards_of in shards:
        steps = jax.random.uniform(jax.random.fold_in(jax.random.fold_in(own_key, 6), axis_at), (shards_of,), jnp.float32, least / len(shards), top_value / len(shards))
        level = level * jnp.repeat(jnp.exp(steps), dims[axis_at] // shards_of).reshape((-1,) + (1,) * (len(dims) - 1 - axis_at))
    return level


def gaussian(stream_key, extent, spread, limit, pieces=(), held_as=jnp.bfloat16):
    result = jax.random.normal(stream_key, extent, jnp.float32) * spread
    if len(pieces) > 0:
        result = level_of(stream_key, extent, pieces, -0.22, 0.18) * result
    return jnp.clip(result, min=-limit, max=limit).astype(held_as)


def setup_inputs(seed: int = 0) -> dict:
    seeds = jax.random.split(jax.random.key(seed), 7)
    state = gaussian(seeds[0], (PARTICLES, 3, NY, COLS), 1.0, 6.0, ((0, 32), (2, 8)), jnp.float32)
    noise = gaussian(seeds[1], (PARTICLES, NY, COLS), 0.3, 4.0, ((0, 32), (1, 8)), jnp.float32)
    parents = draw_parents(jax.random.fold_in(seeds[6], 71), 0)
    measured_cell_position = draw_measured_cell_position(jax.random.fold_in(seeds[6], 71), 0)
    obs_value = gaussian(seeds[4], (OBS,), 1.0, 6.0, ((0, 8),), jnp.float32)
    obs_precision = draw_obs_precision(jax.random.fold_in(seeds[6], 71), 0)
    return dict(state=state, noise=noise, parents=parents, measured_cell_position=measured_cell_position, obs_value=obs_value, obs_precision=obs_precision)


courant = 1.2
coriolis = 0.1
relaxation_gain = 0.3


def column_diff(field):
    return 0.5 * (jnp.roll(field, -1, -1) - jnp.roll(field, 1, -1))


def row_diff(field):
    return 0.5 * (field[..., 2:, :] - field[..., :-2, :])


def advance(free_elevation, zonal_wind_speed, meridional_wind_speed, gain, target):
    height_one = free_elevation[..., 1:-1, :] - courant * (column_diff(zonal_wind_speed)[..., 1:-1, :] + row_diff(meridional_wind_speed))
    eastward_velocity_one = zonal_wind_speed[..., 2:-2, :] + coriolis * meridional_wind_speed[..., 2:-2, :] - courant * column_diff(height_one)[..., 1:-1, :]
    north_one = meridional_wind_speed[..., 2:-2, :] - coriolis * zonal_wind_speed[..., 2:-2, :] - courant * row_diff(height_one)
    centre = height_one[..., 1:-1, :]
    height_two = centre + gain[2:-2] * (target[2:-2] - centre)
    return height_two, eastward_velocity_one, north_one


def reference(state, noise, parents, measured_cell_position, obs_value, obs_precision):
    cells = NY * COLS
    gain = jnp.zeros((cells,), jnp.float32).at[measured_cell_position].set(relaxation_gain).reshape(NY, COLS)
    target = jnp.zeros((cells,), jnp.float32).at[measured_cell_position].set(obs_value).reshape(NY, COLS)
    gain_pad = jnp.pad(gain, ((2, 2), (0, 0)))
    target_pad = jnp.pad(target, ((2, 2), (0, 0)))

    def one_particle(slot):
        parent = parents[slot]
        chosen = state[parent]
        free_elevation = chosen[0] + noise[slot]
        zonal_wind_speed = chosen[1]
        meridional_wind_speed = chosen[2]
        for step in range(STEPS):
            free_elevation, zonal_wind_speed, meridional_wind_speed = advance(
                jnp.pad(free_elevation, ((2, 2), (0, 0))),
                jnp.pad(zonal_wind_speed, ((2, 2), (0, 0))),
                jnp.pad(meridional_wind_speed, ((2, 2), (0, 0))),
                gain_pad, target_pad)
        seen = free_elevation.reshape(-1)[measured_cell_position]
        total = jnp.sum(obs_precision * (obs_value - seen) ** 2)
        return jnp.stack([free_elevation, zonal_wind_speed, meridional_wind_speed], 0), total

    fields, totals = lax.map(one_particle, jnp.arange(PARTICLES, dtype=jnp.int32))
    observation_mismatch = 0.5 * totals / jnp.float32(OBS)
    return fields, observation_mismatch
```

```python
import functools

import jax
import jax.numpy as jnp
from jax import lax
from jax.experimental import pallas as pl
from jax.experimental.pallas import tpu as pltpu
from jax.sharding import PartitionSpec as P

STEPS = 4
LANES = 128
HALO = 8
TALL = 48

COURANT = 1.2
CORIOLIS = 0.1
RELAXATION = 0.3

NOISE, GAIN, FIRST, SECOND = range(4)


def split_three(x):
    high = x.astype(jnp.bfloat16)
    rest = x - high.astype(jnp.float32)
    middle = rest.astype(jnp.bfloat16)
    low = (rest - middle.astype(jnp.float32)).astype(jnp.bfloat16)
    return high, middle, low


def kernel(
    n, tiles, cols, obs, obs_all,
    parents, position, value, precision, state, noise,
    fields_out, mismatch_out,
    every0, every1, every2, pick0, pick1, pick2, fields, noise_all, nudge, weight, row_values, work, result, sums,
    spread_send, spread_recv, local_sem, back_send, back_recv, halo_send, halo_recv, sums_send, sums_recv, out_sem,
):
    every = (every0, every1, every2)
    pick = (pick0, pick1, pick2)
    groups = cols // LANES
    dom = lax.axis_index("dom")
    tile = lax.axis_index("tile")
    has_above = tile > 0
    has_below = tile < tiles - 1

    def place(stage, j):
        column = pl.multiple_of((j % groups) * LANES, LANES)
        if stage == 0:
            field, row = j // (2 * groups), 3 * ((j // groups) % 2)
        elif stage == 1:
            field, row = 2, j // groups
        else:
            field, row = j // (2 * groups), 1 + (j // groups) % 2
        return field, row * 8, column

    def partner(i):
        planes = n // 4
        turn = i // 4
        away = (turn + 1) // 2
        ahead = jnp.where(turn % 2 == 1, away, planes - away)
        z = (dom // 4 + ahead) % planes
        return z * 4 + (dom % 4 + i % 4) % 4

    barrier = pltpu.get_barrier_semaphore()

    @pl.loop(1, n)
    def _(i):
        pl.semaphore_signal(barrier, 1, device_id={"dom": (dom + i) % n})

    @pl.loop(1, tiles)
    def _(i):
        pl.semaphore_signal(barrier, 1, device_id={"tile": (tile + i) % tiles})

    noise_copy = pltpu.make_async_copy(noise, noise_all.at[:, HALO:HALO + 32, :], local_sem.at[0])
    noise_copy.start()
    pl.semaphore_wait(barrier, n - 1 + tiles - 1)

    def spread(stage):
        def piece(j):
            field, row, column = place(stage, j)
            return state.at[:, field, pl.ds(pl.multiple_of(row, 8), 8), pl.ds(column, LANES)]

        mine = every[stage].at[pl.ds(2 * dom, 2)]

        @pl.loop(1, n)
        def _(i):
            target = partner(i)
            pltpu.make_async_remote_copy(
                piece(target), mine, spread_send.at[stage], spread_recv.at[stage], device_id={"dom": target}
            ).start()

        pltpu.make_async_copy(piece(dom), mine, spread_recv.at[stage]).start()

    def give_back(stage, first, count, sem):
        field, row, column = place(stage, dom)
        rows, lanes = pl.ds(pl.multiple_of(row, 8), 8), pl.ds(column, LANES)
        rows = pl.ds(pl.multiple_of(HALO + row, 8), 8)
        there = fields.at[pl.ds(first, count), field, rows, lanes]

        @pl.loop(1, n)
        def _(i):
            target = partner(i)
            pltpu.make_async_remote_copy(
                pick[stage].at[pl.ds(2 * target + first, count)], there,
                back_send.at[sem], back_recv.at[sem], device_id={"dom": target},
            ).start()

        pltpu.make_async_copy(pick[stage].at[pl.ds(2 * dom + first, count)], there, back_recv.at[sem]).start()

    def choose(stage):
        pltpu.make_async_copy(every[stage], every[stage], spread_recv.at[stage]).wait()

        @pl.loop(0, 2 * n, unroll=8)
        def _(s):
            pick[stage][s] = every[stage][parents[s]]

    def await_back(sem, count):
        whole = pick[0].at[pl.ds(0, count * n)]
        pltpu.make_async_copy(whole, whole, back_recv.at[sem]).wait()

    def to_above(kind, source, there):
        return pltpu.make_async_remote_copy(
            source, there, halo_send.at[kind, 0], halo_recv.at[kind, 0], device_id={"tile": jnp.maximum(tile - 1, 0)}
        )

    def to_below(kind, source, there):
        return pltpu.make_async_remote_copy(
            source, there, halo_send.at[kind, 1], halo_recv.at[kind, 1],
            device_id={"tile": jnp.minimum(tile + 1, tiles - 1)},
        )

    top, bottom = pl.ds(HALO, HALO), pl.ds(HALO + 24, HALO)
    over, under = pl.ds(0, HALO), pl.ds(HALO + 32, HALO)

    def halos(kind):
        if kind == NOISE:
            up = to_above(kind, noise.at[:, pl.ds(0, HALO), :], noise_all.at[:, under, :])
            down = to_below(kind, noise.at[:, pl.ds(24, HALO), :], noise_all.at[:, over, :])
        elif kind == GAIN:
            up = to_above(kind, nudge.at[:, top, :], nudge.at[:, under, :])
            down = to_below(kind, nudge.at[:, bottom, :], nudge.at[:, over, :])
        else:
            which = pl.ds(0, 2) if kind == FIRST else pl.ds(2, 1)
            up = to_above(kind, fields.at[:, which, top, :], fields.at[:, which, under, :])
            down = to_below(kind, fields.at[:, which, bottom, :], fields.at[:, which, over, :])
        return up, down

    def send_halo(kind):
        up, down = halos(kind)

        @pl.when(has_above)
        def _():
            up.start()

        @pl.when(has_below)
        def _():
            down.start()

    def await_halo(kind):
        up, down = halos(kind)

        @pl.when(has_below)
        def _():
            up.wait_recv()

        @pl.when(has_above)
        def _():
            down.wait_recv()

    def await_halo_sent(kind):
        up, down = halos(kind)

        @pl.when(has_above)
        def _():
            up.wait_send()

        @pl.when(has_below)
        def _():
            down.wait_send()

    spread(0)
    spread(1)
    send_halo(NOISE)

    @pl.when(tile == 0)
    def _():
        fields[:, :, 0:HALO, :] = jnp.zeros((2, 3, HALO, cols), jnp.float32)
        noise_all[:, 0:HALO, :] = jnp.zeros((2, HALO, cols), jnp.float32)
        nudge[:, 0:HALO, :] = jnp.zeros((2, HALO, cols), jnp.float32)

    @pl.when(tile == tiles - 1)
    def _():
        fields[:, :, HALO + 32:, :] = jnp.zeros((2, 3, HALO, cols), jnp.float32)
        noise_all[:, HALO + 32:, :] = jnp.zeros((2, HALO, cols), jnp.float32)
        nudge[:, HALO + 32:, :] = jnp.zeros((2, HALO, cols), jnp.float32)

    local = position[...] - tile * (32 * cols)
    row_of = local // cols
    column_of = local % cols
    in_row = lax.broadcasted_iota(jnp.int32, (32, obs), 0) == row_of

    def put(slot, row):
        spread_row = jnp.where(in_row, row.astype(jnp.float32), 0.0)
        row_values[slot * 32:(slot + 1) * 32, :] = spread_row.astype(jnp.bfloat16)

    put(0, jnp.ones((1, obs), jnp.float32))
    for at, part in enumerate(split_three(value[...])):
        put(1 + at, part)
    for at, part in enumerate(split_three(precision[...])):
        put(4 + at, part)

    wide = min(cols, 256)

    @pl.loop(0, cols // wide)
    def _(block):
        first = pl.multiple_of(block * wide, wide)
        column = lax.broadcasted_iota(jnp.int32, (wide, obs), 0) + first
        in_column = jnp.where(column == column_of, 1.0, 0.0).astype(jnp.bfloat16)
        grid = lax.dot_general(
            row_values[...], in_column, (((1,), (1,)), ((), ())), preferred_element_type=jnp.float32
        )
        lanes = pl.ds(first, wide)
        nudge[0, HALO:HALO + 32, lanes] = RELAXATION * grid[0:32]
        nudge[1, HALO:HALO + 32, lanes] = (grid[32:64] + grid[64:96]) + grid[96:128]
        weight[:, lanes] = (grid[128:160] + grid[160:192]) + grid[192:224]

    send_halo(GAIN)

    choose(0)
    give_back(0, 0, 2, 0)
    spread(2)
    choose(1)
    give_back(1, 0, 2, 1)
    await_back(0, 2)
    send_halo(FIRST)
    choose(2)
    give_back(2, 0, 1, 2)
    give_back(2, 1, 1, 3)
    await_back(1, 2)
    send_halo(SECOND)

    noise_copy.wait()
    for kind in range(4):
        await_halo(kind)

    row_id = lax.broadcasted_iota(jnp.int32, (TALL, cols), 0)
    inside = jnp.logical_and(
        jnp.logical_or(row_id >= HALO, has_above), jnp.logical_or(row_id < HALO + 32, has_below)
    )

    def column_change(a):
        return pltpu.roll(a, cols - 1, 1) - pltpu.roll(a, 1, 1)

    def row_change(a):
        return pltpu.roll(a, TALL - 1, 0) - pltpu.roll(a, 1, 0)

    half = 0.5 * COURANT

    def forecast(p):
        for step in range(STEPS):
            if step == 0:
                h, u, v = fields[p, 0] + noise_all[p], fields[p, 1], fields[p, 2]
            else:
                h, u, v = work[0], work[1], work[2]
            h1 = h - half * (column_change(u) + row_change(v))
            u1 = u + CORIOLIS * v - half * column_change(h1)
            v1 = v - CORIOLIS * u - half * row_change(h1)
            h2 = h1 + nudge[0] * (nudge[1] - h1)
            if step < STEPS - 1:
                work[0] = jnp.where(inside, h2, 0.0)
                work[1] = jnp.where(inside, u1, 0.0)
                work[2] = jnp.where(inside, v1, 0.0)
            else:
                h2 = h2[HALO:HALO + 32]
                result[p, 0] = h2
                result[p, 1] = u1[HALO:HALO + 32]
                result[p, 2] = v1[HALO:HALO + 32]
                miss = nudge[1, HALO:HALO + 32, :] - h2
                miss = weight[...] * (miss * miss)
                total = jnp.zeros((8, LANES), jnp.float32)
                for r in range(4):
                    for c in range(groups):
                        total = total + miss[8 * r:8 * r + 8, LANES * c:LANES * (c + 1)]
                sums[tile, p] = total
        pltpu.make_async_copy(result.at[p], fields_out.at[p], out_sem.at[p]).start()

    await_back(2, 1)
    forecast(0)
    await_back(3, 1)
    forecast(1)

    @pl.loop(1, tiles)
    def _(i):
        pltpu.make_async_remote_copy(
            sums.at[tile], sums.at[tile], sums_send, sums_recv, device_id={"tile": (tile + i) % tiles}
        ).start()

    others = sums.at[pl.ds(0, tiles - 1)]
    pltpu.make_async_copy(others, others, sums_recv).wait()
    total = sums[0]
    for t in range(1, tiles):
        total = total + sums[t]
    for p in range(2):
        mismatch_out[p] = 0.5 * jnp.sum(total[p]) / jnp.float32(obs_all)

    for p in range(2):
        pltpu.make_async_copy(result.at[p], fields_out.at[p], out_sem.at[p]).wait()
    pltpu.make_async_copy(others, others, sums_send).wait()
    two = pick[0].at[pl.ds(0, 2 * (n - 1))]
    one = pick[0].at[pl.ds(0, n - 1)]
    for stage in range(3):
        pltpu.make_async_copy(two, two, spread_send.at[stage]).wait()
    for sem in range(4):
        sent = two if sem < 2 else one
        pltpu.make_async_copy(sent, sent, back_send.at[sem]).wait()
    for kind in range(4):
        await_halo_sent(kind)


def body(state, noise, parents, measured_cell_position, obs_value, obs_precision):
    n, tiles = lax.axis_size("dom"), lax.axis_size("tile")
    cols = state.shape[3]
    obs = measured_cell_position.shape[0]
    f32 = jnp.float32
    vmem = pl.BlockSpec(memory_space=pltpu.VMEM)
    smem = pl.BlockSpec(memory_space=pltpu.SMEM)
    hbm = pl.BlockSpec(memory_space=pl.ANY)
    dma = pltpu.SemaphoreType.DMA
    pieces = pltpu.VMEM((2 * n, 8, LANES), f32)
    return pl.pallas_call(
        functools.partial(kernel, n, tiles, cols, obs, obs * tiles),
        out_shape=(
            jax.ShapeDtypeStruct(state.shape, f32),
            jax.ShapeDtypeStruct((2,), f32),
        ),
        in_specs=[smem, vmem, vmem, vmem, hbm, hbm],
        out_specs=(hbm, smem),
        scratch_shapes=[
            pieces, pieces, pieces, pieces, pieces, pieces,
            pltpu.VMEM((2, 3, TALL, cols), f32),
            pltpu.VMEM((2, TALL, cols), f32),
            pltpu.VMEM((2, TALL, cols), f32),
            pltpu.VMEM((32, cols), f32),
            pltpu.VMEM((7 * 32, obs), jnp.bfloat16),
            pltpu.VMEM((3, TALL, cols), f32),
            pltpu.VMEM((2, 3, 32, cols), f32),
            pltpu.VMEM((tiles, 2, 8, LANES), f32),
            dma((3,)), dma((3,)), dma((1,)), dma((4,)), dma((4,)),
            dma((4, 2)), dma((4, 2)), dma, dma, dma((2,)),
        ],
        compiler_params=pltpu.CompilerParams(
            collective_id=0, has_side_effects=True, vmem_limit_bytes=48 * 1024 * 1024
        ),
    )(
        parents,
        measured_cell_position.reshape(1, obs),
        obs_value.reshape(1, obs),
        obs_precision.reshape(1, obs),
        state,
        noise,
    )


def solution(mesh):
    placed = (
        P("dom", None, "tile", None),
        P("dom", "tile", None),
        P(),
        P("tile"),
        P("tile"),
        P("tile"),
    )
    return jax.shard_map(
        body,
        mesh=mesh,
        in_specs=placed,
        out_specs=(P("dom", None, "tile", None), P("dom")),
        check_vma=False,
    )
```

```python
import functools

import jax
import jax.numpy as jnp
from jax import lax
from jax.experimental import pallas as pl
from jax.experimental.pallas import tpu as pltpu
from jax.sharding import PartitionSpec as P

STEPS = 4
LANES = 128
HALO = 8
TALL = 48

COURANT = 1.2
CORIOLIS = 0.1
RELAXATION = 0.3

NOISE, GAIN, FIRST, SECOND = range(4)


def split_three(x):
    high = x.astype(jnp.bfloat16)
    rest = x - high.astype(jnp.float32)
    middle = rest.astype(jnp.bfloat16)
    low = (rest - middle.astype(jnp.float32)).astype(jnp.bfloat16)
    return high, middle, low


def kernel(
    n, tiles, cols, obs,
    parents_in, position_in, value_in, precision_in, state, noise,
    fields_out, mismatch_out,
    parents, position, value, precision,
    every0, every1, every2, pick0, pick1, pick2, fields, noise_all, nudge, weight, row_values, work, result, sums,
    spread_send, spread_recv, local_sem, back_send, back_recv, halo_send, halo_recv, sums_send, sums_recv, out_sem,
):
    every = (every0, every1, every2)
    pick = (pick0, pick1, pick2)
    groups = cols // LANES
    dom = lax.axis_index("dom")
    tile = lax.axis_index("tile")
    has_above = tile > 0
    has_below = tile < tiles - 1

    def place(stage, j):
        column = pl.multiple_of((j % groups) * LANES, LANES)
        if stage == 0:
            field, row = j // (2 * groups), 3 * ((j // groups) % 2)
        elif stage == 1:
            field, row = 2, j // groups
        else:
            field, row = j // (2 * groups), 1 + (j // groups) % 2
        return field, row * 8, column

    def partner(i):
        planes = n // 4
        turn = i // 4
        away = (turn + 1) // 2
        ahead = jnp.where(turn % 2 == 1, away, planes - away)
        z = (dom // 4 + ahead) % planes
        return z * 4 + (dom % 4 + i % 4) % 4

    barrier = pltpu.get_barrier_semaphore()

    for i in range(n - 1, 0, -1):
        pl.semaphore_signal(barrier, 1, device_id={"dom": partner(i)})
    for i in range(1, tiles):
        pl.semaphore_signal(barrier, 1, device_id={"tile": (tile + i) % tiles})

    noise_copy = pltpu.make_async_copy(noise, noise_all.at[:, HALO:HALO + 32, :], local_sem.at[0])
    small_copies = [
        pltpu.make_async_copy(source, there, local_sem.at[1 + at])
        for at, (source, there) in enumerate(
            ((parents_in, parents), (position_in, position), (value_in, value), (precision_in, precision))
        )
    ]
    for copy in small_copies:
        copy.start()
    noise_copy.start()
    pl.semaphore_wait(barrier, n - 1 + tiles - 1)

    def spread(stage):
        def piece(j):
            field, row, column = place(stage, j)
            return state.at[:, field, pl.ds(pl.multiple_of(row, 8), 8), pl.ds(column, LANES)]

        mine = every[stage].at[pl.ds(2 * dom, 2)]

        @pl.loop(1, n)
        def _(i):
            target = partner(i)
            pltpu.make_async_remote_copy(
                piece(target), mine, spread_send.at[stage], spread_recv.at[stage], device_id={"dom": target}
            ).start()

        pltpu.make_async_copy(piece(dom), mine, spread_recv.at[stage]).start()

    def give_back(stage, first, count, sem):
        field, row, column = place(stage, dom)
        rows, lanes = pl.ds(pl.multiple_of(row, 8), 8), pl.ds(column, LANES)
        rows = pl.ds(pl.multiple_of(HALO + row, 8), 8)
        there = fields.at[pl.ds(first, count), field, rows, lanes]

        @pl.loop(1, n)
        def _(i):
            target = partner(i)
            pltpu.make_async_remote_copy(
                pick[stage].at[pl.ds(2 * target + first, count)], there,
                back_send.at[sem], back_recv.at[sem], device_id={"dom": target},
            ).start()

        pltpu.make_async_copy(pick[stage].at[pl.ds(2 * dom + first, count)], there, back_recv.at[sem]).start()

    def choose(stage):
        pltpu.make_async_copy(every[stage], every[stage], spread_recv.at[stage]).wait()

        @pl.loop(0, 2 * n, unroll=8)
        def _(s):
            pick[stage][s] = every[stage][parents[s]]

    def await_back(sem, count):
        whole = pick[0].at[pl.ds(0, count * n)]
        pltpu.make_async_copy(whole, whole, back_recv.at[sem]).wait()

    def to_above(kind, source, there):
        return pltpu.make_async_remote_copy(
            source, there, halo_send.at[kind, 0], halo_recv.at[kind, 0], device_id={"tile": jnp.maximum(tile - 1, 0)}
        )

    def to_below(kind, source, there):
        return pltpu.make_async_remote_copy(
            source, there, halo_send.at[kind, 1], halo_recv.at[kind, 1],
            device_id={"tile": jnp.minimum(tile + 1, tiles - 1)},
        )

    top, bottom = pl.ds(HALO, HALO), pl.ds(HALO + 24, HALO)
    over, under = pl.ds(0, HALO), pl.ds(HALO + 32, HALO)

    def halos(kind):
        if kind == NOISE:
            up = to_above(kind, noise.at[:, pl.ds(0, HALO), :], noise_all.at[:, under, :])
            down = to_below(kind, noise.at[:, pl.ds(24, HALO), :], noise_all.at[:, over, :])
        elif kind == GAIN:
            up = to_above(kind, nudge.at[:, top, :], nudge.at[:, under, :])
            down = to_below(kind, nudge.at[:, bottom, :], nudge.at[:, over, :])
        else:
            which = pl.ds(0, 2) if kind == FIRST else pl.ds(2, 1)
            up = to_above(kind, fields.at[:, which, top, :], fields.at[:, which, under, :])
            down = to_below(kind, fields.at[:, which, bottom, :], fields.at[:, which, over, :])
        return up, down

    def send_halo(kind):
        up, down = halos(kind)

        @pl.when(has_above)
        def _():
            up.start()

        @pl.when(has_below)
        def _():
            down.start()

    def await_halo(kind):
        up, down = halos(kind)

        @pl.when(has_below)
        def _():
            up.wait_recv()

        @pl.when(has_above)
        def _():
            down.wait_recv()

    def await_halo_sent(kind):
        up, down = halos(kind)

        @pl.when(has_above)
        def _():
            up.wait_send()

        @pl.when(has_below)
        def _():
            down.wait_send()

    spread(0)
    spread(1)
    send_halo(NOISE)

    @pl.when(tile == 0)
    def _():
        fields[:, :, 0:HALO, :] = jnp.zeros((2, 3, HALO, cols), jnp.float32)
        noise_all[:, 0:HALO, :] = jnp.zeros((2, HALO, cols), jnp.float32)
        nudge[:, 0:HALO, :] = jnp.zeros((2, HALO, cols), jnp.float32)

    @pl.when(tile == tiles - 1)
    def _():
        fields[:, :, HALO + 32:, :] = jnp.zeros((2, 3, HALO, cols), jnp.float32)
        noise_all[:, HALO + 32:, :] = jnp.zeros((2, HALO, cols), jnp.float32)
        nudge[:, HALO + 32:, :] = jnp.zeros((2, HALO, cols), jnp.float32)

    for copy in small_copies:
        copy.wait()

    local = position[...] - tile * (32 * cols)
    row_of = local // cols
    column_of = local % cols
    in_row = lax.broadcasted_iota(jnp.int32, (32, obs), 0) == row_of

    def put(slot, row):
        spread_row = jnp.where(in_row, row.astype(jnp.float32), 0.0)
        row_values[slot * 32:(slot + 1) * 32, :] = spread_row.astype(jnp.bfloat16)

    put(0, jnp.ones((1, obs), jnp.float32))
    for at, part in enumerate(split_three(value[...])):
        put(1 + at, part)
    for at, part in enumerate(split_three(precision[...])):
        put(4 + at, part)

    wide = min(cols, 256)

    @pl.loop(0, cols // wide)
    def _(block):
        first = pl.multiple_of(block * wide, wide)
        column = lax.broadcasted_iota(jnp.int32, (wide, obs), 0) + first
        in_column = jnp.where(column == column_of, 1.0, 0.0).astype(jnp.bfloat16)
        grid = lax.dot_general(
            row_values[...], in_column, (((1,), (1,)), ((), ())), preferred_element_type=jnp.float32
        )
        lanes = pl.ds(first, wide)
        nudge[0, HALO:HALO + 32, lanes] = RELAXATION * grid[0:32]
        nudge[1, HALO:HALO + 32, lanes] = (grid[32:64] + grid[64:96]) + grid[96:128]
        weight[:, lanes] = (grid[128:160] + grid[160:192]) + grid[192:224]

    send_halo(GAIN)

    choose(0)
    give_back(0, 0, 2, 0)
    spread(2)
    choose(1)
    give_back(1, 0, 2, 1)
    await_back(0, 2)
    send_halo(FIRST)
    choose(2)
    give_back(2, 0, 1, 2)
    give_back(2, 1, 1, 3)
    await_back(1, 2)
    send_halo(SECOND)

    noise_copy.wait()
    for kind in range(4):
        await_halo(kind)

    row_id = lax.broadcasted_iota(jnp.int32, (TALL, cols), 0)
    inside = jnp.logical_and(
        jnp.logical_or(row_id >= HALO, has_above), jnp.logical_or(row_id < HALO + 32, has_below)
    )

    def column_change(a):
        return pltpu.roll(a, cols - 1, 1) - pltpu.roll(a, 1, 1)

    def row_change(a):
        return pltpu.roll(a, TALL - 1, 0) - pltpu.roll(a, 1, 0)

    half = 0.5 * COURANT

    def sums_copy(p, i):
        mine = sums.at[p, tile]
        return pltpu.make_async_remote_copy(
            mine, mine, sums_send.at[p], sums_recv.at[p], device_id={"tile": (tile + i) % tiles}
        )

    def forecast(p):
        for step in range(STEPS):
            if step == 0:
                h, u, v = fields[p, 0] + noise_all[p], fields[p, 1], fields[p, 2]
            else:
                h, u, v = work[0], work[1], work[2]
            h1 = h - half * (column_change(u) + row_change(v))
            h2 = h1 + nudge[0] * (nudge[1] - h1)
            if step == STEPS - 1:
                h2 = h2[HALO:HALO + 32]
                miss = nudge[1, HALO:HALO + 32, :] - h2
                miss = weight[...] * (miss * miss)
                total = jnp.zeros((8, LANES), jnp.float32)
                for r in range(4):
                    for c in range(groups):
                        total = total + miss[8 * r:8 * r + 8, LANES * c:LANES * (c + 1)]
                sums[p, tile] = total
                for i in range(1, tiles):
                    sums_copy(p, i).start()
            u1 = u + CORIOLIS * v - half * column_change(h1)
            v1 = v - CORIOLIS * u - half * row_change(h1)
            if step < STEPS - 1:
                work[0] = jnp.where(inside, h2, 0.0)
                work[1] = jnp.where(inside, u1, 0.0)
                work[2] = jnp.where(inside, v1, 0.0)
            else:
                result[p, 0] = h2
                result[p, 1] = u1[HALO:HALO + 32]
                result[p, 2] = v1[HALO:HALO + 32]
        pltpu.make_async_copy(result.at[p], fields_out.at[p], out_sem.at[p]).start()

    await_back(2, 1)
    forecast(0)
    await_back(3, 1)
    forecast(1)

    for p in range(2):
        others = sums.at[p, pl.ds(0, tiles - 1)]
        pltpu.make_async_copy(others, others, sums_recv.at[p]).wait()
        total = sums[p, 0]
        for t in range(1, tiles):
            total = total + sums[p, t]
        mismatch_out[p] = total

    for p in range(2):
        pltpu.make_async_copy(result.at[p], fields_out.at[p], out_sem.at[p]).wait()
        others = sums.at[p, pl.ds(0, tiles - 1)]
        pltpu.make_async_copy(others, others, sums_send.at[p]).wait()
    two = pick[0].at[pl.ds(0, 2 * (n - 1))]
    one = pick[0].at[pl.ds(0, n - 1)]
    for stage in range(3):
        pltpu.make_async_copy(two, two, spread_send.at[stage]).wait()
    for sem in range(4):
        sent = two if sem < 2 else one
        pltpu.make_async_copy(sent, sent, back_send.at[sem]).wait()
    for kind in range(4):
        await_halo_sent(kind)


def body(state, noise, parents, measured_cell_position, obs_value, obs_precision):
    n, tiles = lax.axis_size("dom"), lax.axis_size("tile")
    cols = state.shape[3]
    obs = measured_cell_position.shape[0]
    f32 = jnp.float32
    vmem = pl.BlockSpec(memory_space=pltpu.VMEM)
    hbm = pl.BlockSpec(memory_space=pltpu.HBM)
    somewhere = pl.BlockSpec(memory_space=pl.ANY)
    dma = pltpu.SemaphoreType.DMA
    pieces = pltpu.VMEM((2 * n, 8, LANES), f32)
    fields, sums = pl.pallas_call(
        functools.partial(kernel, n, tiles, cols, obs),
        out_shape=(
            jax.ShapeDtypeStruct(state.shape, f32),
            jax.ShapeDtypeStruct((2, 8, LANES), f32),
        ),
        in_specs=[hbm] * 6,
        out_specs=(somewhere, vmem),
        scratch_shapes=[
            pltpu.SMEM((2 * n,), jnp.int32),
            pltpu.VMEM((1, obs), jnp.int32),
            pltpu.VMEM((1, obs), f32),
            pltpu.VMEM((1, obs), f32),
            pieces, pieces, pieces, pieces, pieces, pieces,
            pltpu.VMEM((2, 3, TALL, cols), f32),
            pltpu.VMEM((2, TALL, cols), f32),
            pltpu.VMEM((2, TALL, cols), f32),
            pltpu.VMEM((32, cols), f32),
            pltpu.VMEM((7 * 32, obs), jnp.bfloat16),
            pltpu.VMEM((3, TALL, cols), f32),
            pltpu.VMEM((2, 3, 32, cols), f32),
            pltpu.VMEM((2, tiles, 8, LANES), f32),
            dma((3,)), dma((3,)), dma((5,)), dma((4,)), dma((4,)),
            dma((4, 2)), dma((4, 2)), dma((2,)), dma((2,)), dma((2,)),
        ],
        compiler_params=pltpu.CompilerParams(
            collective_id=0, has_side_effects=True, vmem_limit_bytes=56 * 1024 * 1024
        ),
    )(
        parents,
        measured_cell_position.reshape(1, obs),
        obs_value.reshape(1, obs),
        obs_precision.reshape(1, obs),
        state,
        noise,
    )
    return fields, 0.5 * jnp.sum(sums, axis=(1, 2)) / jnp.float32(obs * tiles)


def solution(mesh):
    placed = (
        P("dom", None, "tile", None),
        P("dom", "tile", None),
        P(),
        P("tile"),
        P("tile"),
        P("tile"),
    )
    return jax.shard_map(
        body,
        mesh=mesh,
        in_specs=placed,
        out_specs=(P("dom", None, "tile", None), P("dom")),
        check_vma=False,
    )
```

```python
import functools

import jax
import jax.numpy as jnp
from jax import lax
from jax.experimental import pallas as pl
from jax.experimental.pallas import tpu as pltpu
from jax.sharding import PartitionSpec as P

STEPS = 4
LANES = 128
HALO = 8
TALL = 48

COURANT = 1.2
CORIOLIS = 0.1
RELAXATION = 0.3

NOISE, GAIN, FIRST, SECOND = range(4)


def split_three(x):
    high = x.astype(jnp.bfloat16)
    rest = x - high.astype(jnp.float32)
    middle = rest.astype(jnp.bfloat16)
    low = (rest - middle.astype(jnp.float32)).astype(jnp.bfloat16)
    return high, middle, low


def kernel(
    n, tiles, cols, obs, obs_all,
    parents_in, position_in, value_in, precision_in, state, noise,
    result, mismatch_out,
    parents, position, value, precision,
    every0, every1, every2, pick0, pick1, pick2, fields, noise_all, nudge, weight, row_values, work, sums,
    spread_send, spread_recv, local_sem, back_send, back_recv, halo_send, halo_recv, sums_send, sums_recv,
):
    every = (every0, every1, every2)
    pick = (pick0, pick1, pick2)
    groups = cols // LANES
    dom = lax.axis_index("dom")
    tile = lax.axis_index("tile")
    has_above = tile > 0
    has_below = tile < tiles - 1

    def place(stage, j):
        column = pl.multiple_of((j % groups) * LANES, LANES)
        if stage == 0:
            field, row = j // (2 * groups), 3 * ((j // groups) % 2)
        elif stage == 1:
            field, row = 2, j // groups
        else:
            field, row = j // (2 * groups), 1 + (j // groups) % 2
        return field, row * 8, column

    def partner(i):
        planes = n // 4
        turn = i // 4
        away = (turn + 1) // 2
        ahead = jnp.where(turn % 2 == 1, away, planes - away)
        z = (dom // 4 + ahead) % planes
        return z * 4 + (dom % 4 + i % 4) % 4

    barrier = pltpu.get_barrier_semaphore()

    for i in range(n - 1, 0, -1):
        pl.semaphore_signal(barrier, 1, device_id={"dom": partner(i)})
    for i in range(1, tiles):
        pl.semaphore_signal(barrier, 1, device_id={"tile": (tile + i) % tiles})

    noise_copy = pltpu.make_async_copy(noise, noise_all.at[:, HALO:HALO + 32, :], local_sem.at[0])
    small_copies = [
        pltpu.make_async_copy(source, there, local_sem.at[1 + at])
        for at, (source, there) in enumerate(
            ((parents_in, parents), (position_in, position), (value_in, value), (precision_in, precision))
        )
    ]
    for copy in small_copies:
        copy.start()
    noise_copy.start()
    pl.semaphore_wait(barrier, n - 1 + tiles - 1)

    def spread(stage):
        def piece(j):
            field, row, column = place(stage, j)
            return state.at[:, field, pl.ds(pl.multiple_of(row, 8), 8), pl.ds(column, LANES)]

        mine = every[stage].at[pl.ds(2 * dom, 2)]

        @pl.loop(1, n)
        def _(i):
            target = partner(i)
            pltpu.make_async_remote_copy(
                piece(target), mine, spread_send.at[stage], spread_recv.at[stage], device_id={"dom": target}
            ).start()

        pltpu.make_async_copy(piece(dom), mine, spread_recv.at[stage]).start()

    def give_back(stage, first, count, sem):
        field, row, column = place(stage, dom)
        rows, lanes = pl.ds(pl.multiple_of(row, 8), 8), pl.ds(column, LANES)
        rows = pl.ds(pl.multiple_of(HALO + row, 8), 8)
        there = fields.at[pl.ds(first, count), field, rows, lanes]

        @pl.loop(0, n)
        def _(i):
            target = (i // 4) * 4 + (dom + i) % 4

            @pl.when(target != dom)
            def _():
                pltpu.make_async_remote_copy(
                    pick[stage].at[pl.ds(2 * target + first, count)], there,
                    back_send.at[sem], back_recv.at[sem], device_id={"dom": target},
                ).start()

        pltpu.make_async_copy(pick[stage].at[pl.ds(2 * dom + first, count)], there, back_recv.at[sem]).start()

    def choose(stage):
        pltpu.make_async_copy(every[stage], every[stage], spread_recv.at[stage]).wait()

        @pl.loop(0, 2 * n, unroll=8)
        def _(s):
            pick[stage][s] = every[stage][parents[s]]

    def await_back(sem, count):
        whole = pick[0].at[pl.ds(0, count * n)]
        pltpu.make_async_copy(whole, whole, back_recv.at[sem]).wait()

    def to_above(kind, source, there):
        return pltpu.make_async_remote_copy(
            source, there, halo_send.at[kind, 0], halo_recv.at[kind, 0], device_id={"tile": jnp.maximum(tile - 1, 0)}
        )

    def to_below(kind, source, there):
        return pltpu.make_async_remote_copy(
            source, there, halo_send.at[kind, 1], halo_recv.at[kind, 1],
            device_id={"tile": jnp.minimum(tile + 1, tiles - 1)},
        )

    top, bottom = pl.ds(HALO, HALO), pl.ds(HALO + 24, HALO)
    over, under = pl.ds(0, HALO), pl.ds(HALO + 32, HALO)

    def halos(kind):
        if kind == NOISE:
            up = to_above(kind, noise.at[:, pl.ds(0, HALO), :], noise_all.at[:, under, :])
            down = to_below(kind, noise.at[:, pl.ds(24, HALO), :], noise_all.at[:, over, :])
        elif kind == GAIN:
            up = to_above(kind, nudge.at[:, top, :], nudge.at[:, under, :])
            down = to_below(kind, nudge.at[:, bottom, :], nudge.at[:, over, :])
        else:
            which = pl.ds(0, 2) if kind == FIRST else pl.ds(2, 1)
            up = to_above(kind, fields.at[:, which, top, :], fields.at[:, which, under, :])
            down = to_below(kind, fields.at[:, which, bottom, :], fields.at[:, which, over, :])
        return up, down

    def send_halo(kind):
        up, down = halos(kind)

        @pl.when(has_above)
        def _():
            up.start()

        @pl.when(has_below)
        def _():
            down.start()

    def await_halo(kind):
        up, down = halos(kind)

        @pl.when(has_below)
        def _():
            up.wait_recv()

        @pl.when(has_above)
        def _():
            down.wait_recv()

    def await_halo_sent(kind):
        up, down = halos(kind)

        @pl.when(has_above)
        def _():
            up.wait_send()

        @pl.when(has_below)
        def _():
            down.wait_send()

    spread(0)
    spread(1)
    send_halo(NOISE)

    @pl.when(tile == 0)
    def _():
        fields[:, :, 0:HALO, :] = jnp.zeros((2, 3, HALO, cols), jnp.float32)
        noise_all[:, 0:HALO, :] = jnp.zeros((2, HALO, cols), jnp.float32)
        nudge[:, 0:HALO, :] = jnp.zeros((2, HALO, cols), jnp.float32)

    @pl.when(tile == tiles - 1)
    def _():
        fields[:, :, HALO + 32:, :] = jnp.zeros((2, 3, HALO, cols), jnp.float32)
        noise_all[:, HALO + 32:, :] = jnp.zeros((2, HALO, cols), jnp.float32)
        nudge[:, HALO + 32:, :] = jnp.zeros((2, HALO, cols), jnp.float32)

    for copy in small_copies:
        copy.wait()

    local = position[...] - tile * (32 * cols)
    row_of = local // cols
    column_of = local % cols
    in_row = lax.broadcasted_iota(jnp.int32, (32, obs), 0) == row_of

    def put(slot, row):
        spread_row = jnp.where(in_row, row.astype(jnp.float32), 0.0)
        row_values[slot * 32:(slot + 1) * 32, :] = spread_row.astype(jnp.bfloat16)

    put(0, jnp.ones((1, obs), jnp.float32))
    for at, part in enumerate(split_three(value[...])):
        put(1 + at, part)
    for at, part in enumerate(split_three(precision[...])):
        put(4 + at, part)

    wide = min(cols, 256)

    @pl.loop(0, cols // wide)
    def _(block):
        first = pl.multiple_of(block * wide, wide)
        column = lax.broadcasted_iota(jnp.int32, (wide, obs), 0) + first
        in_column = jnp.where(column == column_of, 1.0, 0.0).astype(jnp.bfloat16)
        grid = lax.dot_general(
            row_values[...], in_column, (((1,), (1,)), ((), ())), preferred_element_type=jnp.float32
        )
        lanes = pl.ds(first, wide)
        nudge[0, HALO:HALO + 32, lanes] = RELAXATION * grid[0:32]
        nudge[1, HALO:HALO + 32, lanes] = (grid[32:64] + grid[64:96]) + grid[96:128]
        weight[:, lanes] = (grid[128:160] + grid[160:192]) + grid[192:224]

    send_halo(GAIN)

    choose(0)
    give_back(0, 0, 2, 0)
    spread(2)
    choose(1)
    give_back(1, 0, 2, 1)
    await_back(0, 2)
    send_halo(FIRST)
    choose(2)
    give_back(2, 0, 1, 2)
    give_back(2, 1, 1, 3)
    await_back(1, 2)
    send_halo(SECOND)

    noise_copy.wait()
    for kind in range(4):
        await_halo(kind)

    row_id = lax.broadcasted_iota(jnp.int32, (TALL, cols), 0)
    inside = jnp.logical_and(
        jnp.logical_or(row_id >= HALO, has_above), jnp.logical_or(row_id < HALO + 32, has_below)
    )

    def column_change(a):
        return pltpu.roll(a, cols - 1, 1) - pltpu.roll(a, 1, 1)

    def row_change(a):
        return pltpu.roll(a, TALL - 1, 0) - pltpu.roll(a, 1, 0)

    half = 0.5 * COURANT

    def sums_copy(p, i):
        mine = sums.at[p, tile]
        return pltpu.make_async_remote_copy(
            mine, mine, sums_send.at[p], sums_recv.at[p], device_id={"tile": (tile + i) % tiles}
        )

    def forecast(p):
        for step in range(STEPS):
            if step == 0:
                h, u, v = fields[p, 0] + noise_all[p], fields[p, 1], fields[p, 2]
            else:
                h, u, v = work[0], work[1], work[2]
            h1 = h - half * (column_change(u) + row_change(v))
            h2 = h1 + nudge[0] * (nudge[1] - h1)
            if step == STEPS - 1:
                h2 = h2[HALO:HALO + 32]
                miss = nudge[1, HALO:HALO + 32, :] - h2
                miss = weight[...] * (miss * miss)
                total = jnp.zeros((8, LANES), jnp.float32)
                for r in range(4):
                    for c in range(groups):
                        total = total + miss[8 * r:8 * r + 8, LANES * c:LANES * (c + 1)]
                sums[p, tile] = total
                for i in sorted(range(1, tiles), key=lambda i: -min(i, tiles - i)):
                    sums_copy(p, i).start()
            u1 = u + CORIOLIS * v - half * column_change(h1)
            v1 = v - CORIOLIS * u - half * row_change(h1)
            if step < STEPS - 1:
                work[0] = jnp.where(inside, h2, 0.0)
                work[1] = jnp.where(inside, u1, 0.0)
                work[2] = jnp.where(inside, v1, 0.0)
            else:
                result[p, 0] = h2
                result[p, 1] = u1[HALO:HALO + 32]
                result[p, 2] = v1[HALO:HALO + 32]

    await_back(2, 1)
    forecast(0)
    await_back(3, 1)
    forecast(1)

    for p in range(2):
        others = sums.at[p, pl.ds(0, tiles - 1)]
        pltpu.make_async_copy(others, others, sums_recv.at[p]).wait()
        total = sums[p, 0]
        for t in range(1, tiles):
            total = total + sums[p, t]
        mismatch_out[p] = total * (0.5 / obs_all)

    for p in range(2):
        others = sums.at[p, pl.ds(0, tiles - 1)]
        pltpu.make_async_copy(others, others, sums_send.at[p]).wait()
    two = pick[0].at[pl.ds(0, 2 * (n - 1))]
    one = pick[0].at[pl.ds(0, n - 1)]
    for stage in range(3):
        pltpu.make_async_copy(two, two, spread_send.at[stage]).wait()
    for sem in range(4):
        sent = two if sem < 2 else one
        pltpu.make_async_copy(sent, sent, back_send.at[sem]).wait()
    for kind in range(4):
        await_halo_sent(kind)


def body(state, noise, parents, measured_cell_position, obs_value, obs_precision):
    n, tiles = lax.axis_size("dom"), lax.axis_size("tile")
    cols = state.shape[3]
    obs = measured_cell_position.shape[0]
    f32 = jnp.float32
    vmem = pl.BlockSpec(memory_space=pltpu.VMEM)
    hbm = pl.BlockSpec(memory_space=pltpu.HBM)
    dma = pltpu.SemaphoreType.DMA
    pieces = pltpu.VMEM((2 * n, 8, LANES), f32)
    fields, sums = pl.pallas_call(
        functools.partial(kernel, n, tiles, cols, obs, obs * tiles),
        out_shape=(
            pltpu.VMEM(state.shape, f32),
            pltpu.VMEM((2, 8, LANES), f32),
        ),
        in_specs=[hbm] * 6,
        out_specs=(vmem, vmem),
        scratch_shapes=[
            pltpu.SMEM((2 * n,), jnp.int32),
            pltpu.VMEM((1, obs), jnp.int32),
            pltpu.VMEM((1, obs), f32),
            pltpu.VMEM((1, obs), f32),
            pieces, pieces, pieces, pieces, pieces, pieces,
            pltpu.VMEM((2, 3, TALL, cols), f32),
            pltpu.VMEM((2, TALL, cols), f32),
            pltpu.VMEM((2, TALL, cols), f32),
            pltpu.VMEM((32, cols), f32),
            pltpu.VMEM((7 * 32, obs), jnp.bfloat16),
            pltpu.VMEM((3, TALL, cols), f32),
            pltpu.VMEM((2, tiles, 8, LANES), f32),
            dma((3,)), dma((3,)), dma((5,)), dma((4,)), dma((4,)),
            dma((4, 2)), dma((4, 2)), dma((2,)), dma((2,)),
        ],
        compiler_params=pltpu.CompilerParams(
            collective_id=0, has_side_effects=True, vmem_limit_bytes=32 * 1024 * 1024
        ),
    )(*(
        pltpu.with_memory_space_constraint(operand, pltpu.HBM)
        for operand in (
            parents,
            measured_cell_position.reshape(1, obs),
            obs_value.reshape(1, obs),
            obs_precision.reshape(1, obs),
            state,
            noise,
        )
    ))
    return fields, jnp.sum(sums, axis=(1, 2))


def solution(mesh):
    placed = (
        P("dom", None, "tile", None),
        P("dom", "tile", None),
        P(),
        P("tile"),
        P("tile"),
        P("tile"),
    )
    return jax.shard_map(
        body,
        mesh=mesh,
        in_specs=placed,
        out_specs=(P("dom", None, "tile", None), P("dom")),
        check_vma=False,
    )
```

```python
import functools

import jax
import jax.numpy as jnp
from jax import lax
from jax.experimental import pallas as pl
from jax.experimental.pallas import tpu as pltpu
from jax.sharding import PartitionSpec as P

STEPS = 4
LANES = 128
HALO = 8
TALL = 48

COURANT = 1.2
CORIOLIS = 0.1
RELAXATION = 0.3

NOISE, GAIN, FIRST, SECOND = range(4)


def split_three(x):
    high = x.astype(jnp.bfloat16)
    rest = x - high.astype(jnp.float32)
    middle = rest.astype(jnp.bfloat16)
    low = (rest - middle.astype(jnp.float32)).astype(jnp.bfloat16)
    return high, middle, low


def kernel(
    n, tiles, cols, obs, obs_all,
    parents_in, position_in, value_in, precision_in, state, noise,
    result, mismatch_out,
    parents, position, value, precision,
    every0, every1, every2, pick0, pick1, pick2, fields, noise_all, nudge, weight, row_values, work, sums,
    spread_send, spread_recv, local_sem, back_send, back_recv, halo_send, halo_recv, sums_send, sums_recv,
):
    every = (every0, every1, every2)
    pick = (pick0, pick1, pick2)
    groups = cols // LANES
    dom = lax.axis_index("dom")
    tile = lax.axis_index("tile")
    has_above = tile > 0
    has_below = tile < tiles - 1

    def place(stage, j):
        column = pl.multiple_of((j % groups) * LANES, LANES)
        if stage == 0:
            field, row = j // (2 * groups), 3 * ((j // groups) % 2)
        elif stage == 1:
            field, row = 2, j // groups
        else:
            field, row = j // (2 * groups), 1 + (j // groups) % 2
        return field, row * 8, column

    def partner(i):
        planes = n // 4
        turn = i // 4
        away = (turn + 1) // 2
        ahead = jnp.where(turn % 2 == 1, away, planes - away)
        z = (dom // 4 + ahead) % planes
        return z * 4 + (dom % 4 + i % 4) % 4

    barrier = pltpu.get_barrier_semaphore()

    for i in range(n - 1, 0, -1):
        pl.semaphore_signal(barrier, 1, device_id={"dom": partner(i)})
    for i in range(1, tiles):
        pl.semaphore_signal(barrier, 1, device_id={"tile": (tile + i) % tiles})

    noise_copy = pltpu.make_async_copy(noise, noise_all.at[:, HALO:HALO + 32, :], local_sem.at[0])
    small_copies = [
        pltpu.make_async_copy(source, there, local_sem.at[1 + at])
        for at, (source, there) in enumerate(
            ((parents_in, parents), (position_in, position), (value_in, value), (precision_in, precision))
        )
    ]
    for copy in small_copies:
        copy.start()
    noise_copy.start()
    pl.semaphore_wait(barrier, n - 1 + tiles - 1)

    def spread(stage):
        def piece(j):
            field, row, column = place(stage, j)
            return state.at[:, field, pl.ds(pl.multiple_of(row, 8), 8), pl.ds(column, LANES)]

        mine = every[stage].at[pl.ds(2 * dom, 2)]

        @pl.loop(1, n)
        def _(i):
            target = partner(i)
            pltpu.make_async_remote_copy(
                piece(target), mine, spread_send.at[stage], spread_recv.at[stage], device_id={"dom": target}
            ).start()

        pltpu.make_async_copy(piece(dom), mine, spread_recv.at[stage]).start()

    def give_back(stage, first, count, sem):
        field, row, column = place(stage, dom)
        rows, lanes = pl.ds(pl.multiple_of(row, 8), 8), pl.ds(column, LANES)
        rows = pl.ds(pl.multiple_of(HALO + row, 8), 8)
        there = fields.at[pl.ds(first, count), field, rows, lanes]

        @pl.loop(0, n)
        def _(i):
            target = (i // 4) * 4 + (dom + i) % 4

            @pl.when(target != dom)
            def _():
                pltpu.make_async_remote_copy(
                    pick[stage].at[pl.ds(2 * target + first, count)], there,
                    back_send.at[sem], back_recv.at[sem], device_id={"dom": target},
                ).start()

        pltpu.make_async_copy(pick[stage].at[pl.ds(2 * dom + first, count)], there, back_recv.at[sem]).start()

    def choose(stage):
        pltpu.make_async_copy(every[stage], every[stage], spread_recv.at[stage]).wait()

        @pl.loop(0, 2 * n, unroll=8)
        def _(s):
            pick[stage][s] = every[stage][parents[s]]

    def await_back(sem, count):
        whole = pick[0].at[pl.ds(0, count * n)]
        pltpu.make_async_copy(whole, whole, back_recv.at[sem]).wait()

    def to_above(kind, source, there):
        return pltpu.make_async_remote_copy(
            source, there, halo_send.at[kind, 0], halo_recv.at[kind, 0], device_id={"tile": jnp.maximum(tile - 1, 0)}
        )

    def to_below(kind, source, there):
        return pltpu.make_async_remote_copy(
            source, there, halo_send.at[kind, 1], halo_recv.at[kind, 1],
            device_id={"tile": jnp.minimum(tile + 1, tiles - 1)},
        )

    top, bottom = pl.ds(HALO, HALO), pl.ds(HALO + 24, HALO)
    over, under = pl.ds(0, HALO), pl.ds(HALO + 32, HALO)

    def halos(kind):
        if kind == NOISE:
            up = to_above(kind, noise.at[:, pl.ds(0, HALO), :], noise_all.at[:, under, :])
            down = to_below(kind, noise.at[:, pl.ds(24, HALO), :], noise_all.at[:, over, :])
        elif kind == GAIN:
            up = to_above(kind, nudge.at[:, top, :], nudge.at[:, under, :])
            down = to_below(kind, nudge.at[:, bottom, :], nudge.at[:, over, :])
        else:
            which = pl.ds(0, 2) if kind == FIRST else pl.ds(2, 1)
            up = to_above(kind, fields.at[:, which, top, :], fields.at[:, which, under, :])
            down = to_below(kind, fields.at[:, which, bottom, :], fields.at[:, which, over, :])
        return up, down

    def send_halo(kind):
        up, down = halos(kind)

        @pl.when(has_above)
        def _():
            up.start()

        @pl.when(has_below)
        def _():
            down.start()

    def await_halo(kind):
        up, down = halos(kind)

        @pl.when(has_below)
        def _():
            up.wait_recv()

        @pl.when(has_above)
        def _():
            down.wait_recv()

    def await_halo_sent(kind):
        up, down = halos(kind)

        @pl.when(has_above)
        def _():
            up.wait_send()

        @pl.when(has_below)
        def _():
            down.wait_send()

    spread(0)
    spread(1)
    send_halo(NOISE)

    @pl.when(tile == 0)
    def _():
        fields[:, :, 0:HALO, :] = jnp.zeros((2, 3, HALO, cols), jnp.float32)
        noise_all[:, 0:HALO, :] = jnp.zeros((2, HALO, cols), jnp.float32)
        nudge[:, 0:HALO, :] = jnp.zeros((2, HALO, cols), jnp.float32)

    @pl.when(tile == tiles - 1)
    def _():
        fields[:, :, HALO + 32:, :] = jnp.zeros((2, 3, HALO, cols), jnp.float32)
        noise_all[:, HALO + 32:, :] = jnp.zeros((2, HALO, cols), jnp.float32)
        nudge[:, HALO + 32:, :] = jnp.zeros((2, HALO, cols), jnp.float32)

    for copy in small_copies:
        copy.wait()

    local = position[...] - tile * (32 * cols)
    row_of = local // cols
    column_of = local % cols
    in_row = lax.broadcasted_iota(jnp.int32, (32, obs), 0) == row_of

    def put(slot, row):
        spread_row = jnp.where(in_row, row.astype(jnp.float32), 0.0)
        row_values[slot * 32:(slot + 1) * 32, :] = spread_row.astype(jnp.bfloat16)

    put(0, jnp.ones((1, obs), jnp.float32))
    for at, part in enumerate(split_three(value[...])):
        put(1 + at, part)
    for at, part in enumerate(split_three(precision[...])):
        put(4 + at, part)

    wide = min(cols, 256)

    @pl.loop(0, cols // wide)
    def _(block):
        first = pl.multiple_of(block * wide, wide)
        column = lax.broadcasted_iota(jnp.int32, (wide, obs), 0) + first
        in_column = jnp.where(column == column_of, 1.0, 0.0).astype(jnp.bfloat16)
        grid = lax.dot_general(
            row_values[...], in_column, (((1,), (1,)), ((), ())), preferred_element_type=jnp.float32
        )
        lanes = pl.ds(first, wide)
        nudge[0, HALO:HALO + 32, lanes] = RELAXATION * grid[0:32]
        nudge[1, HALO:HALO + 32, lanes] = (grid[32:64] + grid[64:96]) + grid[96:128]
        weight[:, lanes] = (grid[128:160] + grid[160:192]) + grid[192:224]

    send_halo(GAIN)

    choose(0)
    give_back(0, 0, 2, 0)
    spread(2)
    choose(1)
    give_back(1, 0, 2, 1)
    await_back(0, 2)
    send_halo(FIRST)
    choose(2)
    give_back(2, 0, 1, 2)
    give_back(2, 1, 1, 3)
    await_back(1, 2)
    send_halo(SECOND)

    noise_copy.wait()
    for kind in range(4):
        await_halo(kind)

    row_id = lax.broadcasted_iota(jnp.int32, (TALL, cols), 0)
    inside = jnp.logical_and(
        jnp.logical_or(row_id >= HALO, has_above), jnp.logical_or(row_id < HALO + 32, has_below)
    )

    def column_change(a):
        return pltpu.roll(a, cols - 1, 1) - pltpu.roll(a, 1, 1)

    def row_change(a):
        return pltpu.roll(a, TALL - 1, 0) - pltpu.roll(a, 1, 0)

    half = 0.5 * COURANT

    def sums_copy(p, i):
        mine = sums.at[p, tile]
        return pltpu.make_async_remote_copy(
            mine, mine, sums_send.at[p], sums_recv.at[p], device_id={"tile": (tile + i) % tiles}
        )

    def forecast(p):
        for step in range(STEPS):
            if step == 0:
                h, u, v = fields[p, 0] + noise_all[p], fields[p, 1], fields[p, 2]
            else:
                h, u, v = work[0], work[1], work[2]
            h1 = h - half * (column_change(u) + row_change(v))
            h2 = h1 + nudge[0] * (nudge[1] - h1)
            if step == STEPS - 1:
                h2 = h2[HALO:HALO + 32]
                miss = nudge[1, HALO:HALO + 32, :] - h2
                miss = weight[...] * (miss * miss)
                total = jnp.zeros((8, LANES), jnp.float32)
                for r in range(4):
                    for c in range(groups):
                        total = total + miss[8 * r:8 * r + 8, LANES * c:LANES * (c + 1)]
                sums[p, tile] = total
                for i in sorted(range(1, tiles), key=lambda i: -min(i, tiles - i)):
                    sums_copy(p, i).start()
            u1 = u + CORIOLIS * v - half * column_change(h1)
            v1 = v - CORIOLIS * u - half * row_change(h1)
            if step < STEPS - 1:
                work[0] = jnp.where(inside, h2, 0.0)
                work[1] = jnp.where(inside, u1, 0.0)
                work[2] = jnp.where(inside, v1, 0.0)
            else:
                result[p, 0] = h2
                result[p, 1] = u1[HALO:HALO + 32]
                result[p, 2] = v1[HALO:HALO + 32]

    await_back(2, 1)
    forecast(0)
    await_back(3, 1)
    forecast(1)

    for p in range(2):
        others = sums.at[p, pl.ds(0, tiles - 1)]
        pltpu.make_async_copy(others, others, sums_recv.at[p]).wait()
        total = sums[p, 0]
        for t in range(1, tiles):
            total = total + sums[p, t]
        mismatch_out[p] = total * (0.5 / obs_all)

    for p in range(2):
        others = sums.at[p, pl.ds(0, tiles - 1)]
        pltpu.make_async_copy(others, others, sums_send.at[p]).wait()
    two = pick[0].at[pl.ds(0, 2 * (n - 1))]
    one = pick[0].at[pl.ds(0, n - 1)]
    for stage in range(3):
        pltpu.make_async_copy(two, two, spread_send.at[stage]).wait()
    for sem in range(4):
        sent = two if sem < 2 else one
        pltpu.make_async_copy(sent, sent, back_send.at[sem]).wait()
    for kind in range(4):
        await_halo_sent(kind)


def finish(fields, sums, fields_out, mismatch_out, both, sem):
    copies = [
        pltpu.make_async_copy(fields.at[p, f], fields_out.at[p, f], sem.at[3 * p + f]) for p in range(2) for f in range(3)
    ]
    for copy in copies:
        copy.start()
    for p in range(2):
        both[p] = jnp.sum(sums[p])
    copies.append(pltpu.make_async_copy(both, mismatch_out, sem.at[6]))
    copies[-1].start()
    for copy in copies:
        copy.wait()


def body(state, noise, parents, measured_cell_position, obs_value, obs_precision):
    n, tiles = lax.axis_size("dom"), lax.axis_size("tile")
    cols = state.shape[3]
    obs = measured_cell_position.shape[0]
    f32 = jnp.float32
    vmem = pl.BlockSpec(memory_space=pltpu.VMEM)
    hbm = pl.BlockSpec(memory_space=pltpu.HBM)
    dma = pltpu.SemaphoreType.DMA
    pieces = pltpu.VMEM((2 * n, 8, LANES), f32)
    fields, sums = pl.pallas_call(
        functools.partial(kernel, n, tiles, cols, obs, obs * tiles),
        out_shape=(
            pltpu.VMEM(state.shape, f32),
            pltpu.VMEM((2, 8, LANES), f32),
        ),
        in_specs=[hbm] * 6,
        out_specs=(vmem, vmem),
        scratch_shapes=[
            pltpu.SMEM((2 * n,), jnp.int32),
            pltpu.VMEM((1, obs), jnp.int32),
            pltpu.VMEM((1, obs), f32),
            pltpu.VMEM((1, obs), f32),
            pieces, pieces, pieces, pieces, pieces, pieces,
            pltpu.VMEM((2, 3, TALL, cols), f32),
            pltpu.VMEM((2, TALL, cols), f32),
            pltpu.VMEM((2, TALL, cols), f32),
            pltpu.VMEM((32, cols), f32),
            pltpu.VMEM((7 * 32, obs), jnp.bfloat16),
            pltpu.VMEM((3, TALL, cols), f32),
            pltpu.VMEM((2, tiles, 8, LANES), f32),
            dma((3,)), dma((3,)), dma((5,)), dma((4,)), dma((4,)),
            dma((4, 2)), dma((4, 2)), dma((2,)), dma((2,)),
        ],
        compiler_params=pltpu.CompilerParams(
            collective_id=0, has_side_effects=True, vmem_limit_bytes=32 * 1024 * 1024
        ),
    )(*(
        pltpu.with_memory_space_constraint(operand, pltpu.HBM)
        for operand in (
            parents,
            measured_cell_position.reshape(1, obs),
            obs_value.reshape(1, obs),
            obs_precision.reshape(1, obs),
            state,
            noise,
        )
    ))
    return pl.pallas_call(
        finish,
        out_shape=(jax.ShapeDtypeStruct(state.shape, f32), jax.ShapeDtypeStruct((2,), f32)),
        in_specs=[vmem, vmem],
        out_specs=(hbm, hbm),
        scratch_shapes=[pltpu.SMEM((2,), f32), dma((7,))],
    )(pltpu.with_memory_space_constraint(fields, pltpu.VMEM), pltpu.with_memory_space_constraint(sums, pltpu.VMEM))


def solution(mesh):
    placed = (
        P("dom", None, "tile", None),
        P("dom", "tile", None),
        P(),
        P("tile"),
        P("tile"),
        P("tile"),
    )
    return jax.shard_map(
        body,
        mesh=mesh,
        in_specs=placed,
        out_specs=(P("dom", None, "tile", None), P("dom")),
        check_vma=False,
    )
```

```python
import functools

import jax
import jax.numpy as jnp
from jax import lax
from jax.experimental import pallas as pl
from jax.experimental.pallas import tpu as pltpu
from jax.sharding import PartitionSpec as P

STEPS = 4
LANES = 128
HALO = 8
TALL = 48

COURANT = 1.2
CORIOLIS = 0.1
RELAXATION = 0.3

NOISE, GAIN, FIRST, SECOND = range(4)


def split_three(x):
    high = x.astype(jnp.bfloat16)
    rest = x - high.astype(jnp.float32)
    middle = rest.astype(jnp.bfloat16)
    low = (rest - middle.astype(jnp.float32)).astype(jnp.bfloat16)
    return high, middle, low


def kernel(
    n, tiles, cols, obs, obs_all,
    parents_in, position_in, value_in, precision_in, state, noise,
    result, mismatch_out,
    parents, position, value, precision,
    every0, every1, every2, pick0, pick1, pick2, fields, noise_all, nudge, weight, row_values, work, sums,
    spread_send, spread_recv, local_sem, back_send, back_recv, halo_send, halo_recv, sums_send, sums_recv,
):
    every = (every0, every1, every2)
    pick = (pick0, pick1, pick2)
    groups = cols // LANES
    dom = lax.axis_index("dom")
    tile = lax.axis_index("tile")
    has_above = tile > 0
    has_below = tile < tiles - 1

    def place(stage, j):
        column = pl.multiple_of((j % groups) * LANES, LANES)
        if stage == 0:
            field, row = j // (2 * groups), 3 * ((j // groups) % 2)
        elif stage == 1:
            field, row = 2, j // groups
        else:
            field, row = j // (2 * groups), 1 + (j // groups) % 2
        return field, row * 8, column

    def partner(i):
        planes = n // 4
        turn = i // 4
        away = (turn + 1) // 2
        ahead = jnp.where(turn % 2 == 1, away, planes - away)
        z = (dom // 4 + ahead) % planes
        return z * 4 + (dom % 4 + i % 4) % 4

    barrier = pltpu.get_barrier_semaphore()

    for i in range(n - 1, 0, -1):
        pl.semaphore_signal(barrier, 1, device_id={"dom": partner(i)})
    for i in range(1, tiles):
        pl.semaphore_signal(barrier, 1, device_id={"tile": (tile + i) % tiles})

    noise_copy = pltpu.make_async_copy(noise, noise_all.at[:, HALO:HALO + 32, :], local_sem.at[0])
    small_copies = [
        pltpu.make_async_copy(source, there, local_sem.at[1 + at])
        for at, (source, there) in enumerate(
            ((parents_in, parents), (position_in, position), (value_in, value), (precision_in, precision))
        )
    ]
    for copy in small_copies:
        copy.start()
    noise_copy.start()
    pl.semaphore_wait(barrier, n - 1 + tiles - 1)

    def spread(stage):
        def piece(j):
            field, row, column = place(stage, j)
            return state.at[:, field, pl.ds(pl.multiple_of(row, 8), 8), pl.ds(column, LANES)]

        mine = every[stage].at[pl.ds(2 * dom, 2)]

        @pl.loop(0, n)
        def _(i):
            target = (i // 4) * 4 + (dom + i) % 4

            @pl.when(target != dom)
            def _():
                pltpu.make_async_remote_copy(
                    piece(target), mine, spread_send.at[stage], spread_recv.at[stage], device_id={"dom": target}
                ).start()

        pltpu.make_async_copy(piece(dom), mine, spread_recv.at[stage]).start()

    def await_spread(stage):
        pltpu.make_async_copy(every[stage], every[stage], spread_recv.at[stage]).wait()

    def give_back(stage, first, count, sem):
        field, row, column = place(stage, dom)
        rows, lanes = pl.ds(pl.multiple_of(HALO + row, 8), 8), pl.ds(column, LANES)
        there = fields.at[pl.ds(first, count), field, rows, lanes]

        def choose(target):
            for p in range(first, first + count):
                pick[stage][2 * target + p] = every[stage][parents[2 * target + p]]

        @pl.loop(0, n)
        def _(i):
            target = (i // 4) * 4 + (dom + i) % 4
            choose(target)

            @pl.when(target != dom)
            def _():
                pltpu.make_async_remote_copy(
                    pick[stage].at[pl.ds(2 * target + first, count)], there,
                    back_send.at[sem], back_recv.at[sem], device_id={"dom": target},
                ).start()

        pltpu.make_async_copy(pick[stage].at[pl.ds(2 * dom + first, count)], there, back_recv.at[sem]).start()

    def await_back(sem, count):
        whole = pick[0].at[pl.ds(0, count * n)]
        pltpu.make_async_copy(whole, whole, back_recv.at[sem]).wait()

    def to_above(kind, source, there):
        return pltpu.make_async_remote_copy(
            source, there, halo_send.at[kind, 0], halo_recv.at[kind, 0], device_id={"tile": jnp.maximum(tile - 1, 0)}
        )

    def to_below(kind, source, there):
        return pltpu.make_async_remote_copy(
            source, there, halo_send.at[kind, 1], halo_recv.at[kind, 1],
            device_id={"tile": jnp.minimum(tile + 1, tiles - 1)},
        )

    top, bottom = pl.ds(HALO, HALO), pl.ds(HALO + 24, HALO)
    over, under = pl.ds(0, HALO), pl.ds(HALO + 32, HALO)

    def halos(kind):
        if kind == NOISE:
            up = to_above(kind, noise.at[:, pl.ds(0, HALO), :], noise_all.at[:, under, :])
            down = to_below(kind, noise.at[:, pl.ds(24, HALO), :], noise_all.at[:, over, :])
        elif kind == GAIN:
            up = to_above(kind, nudge.at[:, top, :], nudge.at[:, under, :])
            down = to_below(kind, nudge.at[:, bottom, :], nudge.at[:, over, :])
        else:
            which = pl.ds(0, 2) if kind == FIRST else pl.ds(2, 1)
            up = to_above(kind, fields.at[:, which, top, :], fields.at[:, which, under, :])
            down = to_below(kind, fields.at[:, which, bottom, :], fields.at[:, which, over, :])
        return up, down

    def send_halo(kind):
        up, down = halos(kind)

        @pl.when(has_above)
        def _():
            up.start()

        @pl.when(has_below)
        def _():
            down.start()

    def await_halo(kind):
        up, down = halos(kind)

        @pl.when(has_below)
        def _():
            up.wait_recv()

        @pl.when(has_above)
        def _():
            down.wait_recv()

    def await_halo_sent(kind):
        up, down = halos(kind)

        @pl.when(has_above)
        def _():
            up.wait_send()

        @pl.when(has_below)
        def _():
            down.wait_send()

    spread(0)
    spread(1)
    send_halo(NOISE)

    @pl.when(tile == 0)
    def _():
        fields[:, :, 0:HALO, :] = jnp.zeros((2, 3, HALO, cols), jnp.float32)
        noise_all[:, 0:HALO, :] = jnp.zeros((2, HALO, cols), jnp.float32)
        nudge[:, 0:HALO, :] = jnp.zeros((2, HALO, cols), jnp.float32)

    @pl.when(tile == tiles - 1)
    def _():
        fields[:, :, HALO + 32:, :] = jnp.zeros((2, 3, HALO, cols), jnp.float32)
        noise_all[:, HALO + 32:, :] = jnp.zeros((2, HALO, cols), jnp.float32)
        nudge[:, HALO + 32:, :] = jnp.zeros((2, HALO, cols), jnp.float32)

    for copy in small_copies:
        copy.wait()

    local = position[...] - tile * (32 * cols)
    row_of = local // cols
    column_of = local % cols
    in_row = lax.broadcasted_iota(jnp.int32, (32, obs), 0) == row_of

    def put(slot, row):
        spread_row = jnp.where(in_row, row.astype(jnp.float32), 0.0)
        row_values[slot * 32:(slot + 1) * 32, :] = spread_row.astype(jnp.bfloat16)

    put(0, jnp.ones((1, obs), jnp.float32))
    for at, part in enumerate(split_three(value[...])):
        put(1 + at, part)
    for at, part in enumerate(split_three(precision[...])):
        put(4 + at, part)

    wide = min(cols, 256)

    @pl.loop(0, cols // wide)
    def _(block):
        first = pl.multiple_of(block * wide, wide)
        column = lax.broadcasted_iota(jnp.int32, (wide, obs), 0) + first
        in_column = jnp.where(column == column_of, 1.0, 0.0).astype(jnp.bfloat16)
        grid = lax.dot_general(
            row_values[...], in_column, (((1,), (1,)), ((), ())), preferred_element_type=jnp.float32
        )
        lanes = pl.ds(first, wide)
        nudge[0, HALO:HALO + 32, lanes] = RELAXATION * grid[0:32]
        nudge[1, HALO:HALO + 32, lanes] = (grid[32:64] + grid[64:96]) + grid[96:128]
        weight[:, lanes] = (grid[128:160] + grid[160:192]) + grid[192:224]

    send_halo(GAIN)

    await_spread(0)
    give_back(0, 0, 2, 0)
    spread(2)
    await_spread(1)
    give_back(1, 0, 2, 1)
    await_back(0, 2)
    send_halo(FIRST)
    await_spread(2)
    give_back(2, 0, 1, 2)
    give_back(2, 1, 1, 3)
    await_back(1, 2)
    send_halo(SECOND)

    noise_copy.wait()
    for kind in range(4):
        await_halo(kind)

    row_id = lax.broadcasted_iota(jnp.int32, (TALL, cols), 0)
    inside = jnp.logical_and(
        jnp.logical_or(row_id >= HALO, has_above), jnp.logical_or(row_id < HALO + 32, has_below)
    )

    def column_change(a):
        return pltpu.roll(a, cols - 1, 1) - pltpu.roll(a, 1, 1)

    def row_change(a):
        return pltpu.roll(a, TALL - 1, 0) - pltpu.roll(a, 1, 0)

    half = 0.5 * COURANT

    def sums_copy(p, i):
        mine = sums.at[p, tile]
        return pltpu.make_async_remote_copy(
            mine, mine, sums_send.at[p], sums_recv.at[p], device_id={"tile": (tile + i) % tiles}
        )

    def forecast(p):
        for step in range(STEPS):
            if step == 0:
                h, u, v = fields[p, 0] + noise_all[p], fields[p, 1], fields[p, 2]
            else:
                h, u, v = work[0], work[1], work[2]
            h1 = h - half * (column_change(u) + row_change(v))
            h2 = h1 + nudge[0] * (nudge[1] - h1)
            if step == STEPS - 1:
                h2 = h2[HALO:HALO + 32]
                miss = nudge[1, HALO:HALO + 32, :] - h2
                miss = weight[...] * (miss * miss)
                total = jnp.zeros((8, LANES), jnp.float32)
                for r in range(4):
                    for c in range(groups):
                        total = total + miss[8 * r:8 * r + 8, LANES * c:LANES * (c + 1)]
                sums[p, tile] = total
                for i in sorted(range(1, tiles), key=lambda i: -min(i, tiles - i)):
                    sums_copy(p, i).start()
            u1 = u + CORIOLIS * v - half * column_change(h1)
            v1 = v - CORIOLIS * u - half * row_change(h1)
            if step < STEPS - 1:
                work[0] = jnp.where(inside, h2, 0.0)
                work[1] = jnp.where(inside, u1, 0.0)
                work[2] = jnp.where(inside, v1, 0.0)
            else:
                result[p, 0] = h2
                result[p, 1] = u1[HALO:HALO + 32]
                result[p, 2] = v1[HALO:HALO + 32]

    await_back(2, 1)
    forecast(0)
    await_back(3, 1)
    forecast(1)

    for p in range(2):
        others = sums.at[p, pl.ds(0, tiles - 1)]
        pltpu.make_async_copy(others, others, sums_recv.at[p]).wait()
        total = sums[p, 0]
        for t in range(1, tiles):
            total = total + sums[p, t]
        mismatch_out[p] = total * (0.5 / obs_all)

    for p in range(2):
        others = sums.at[p, pl.ds(0, tiles - 1)]
        pltpu.make_async_copy(others, others, sums_send.at[p]).wait()
    two = pick[0].at[pl.ds(0, 2 * (n - 1))]
    one = pick[0].at[pl.ds(0, n - 1)]
    for stage in range(3):
        pltpu.make_async_copy(two, two, spread_send.at[stage]).wait()
    for sem in range(4):
        sent = two if sem < 2 else one
        pltpu.make_async_copy(sent, sent, back_send.at[sem]).wait()
    for kind in range(4):
        await_halo_sent(kind)


def finish(fields, sums, fields_out, mismatch_out, both, sem):
    copies = [
        pltpu.make_async_copy(fields.at[p, f], fields_out.at[p, f], sem.at[3 * p + f]) for p in range(2) for f in range(3)
    ]
    for copy in copies:
        copy.start()
    for p in range(2):
        both[p] = jnp.sum(sums[p])
    copies.append(pltpu.make_async_copy(both, mismatch_out, sem.at[6]))
    copies[-1].start()
    for copy in copies:
        copy.wait()


def body(state, noise, parents, measured_cell_position, obs_value, obs_precision):
    n, tiles = lax.axis_size("dom"), lax.axis_size("tile")
    cols = state.shape[3]
    obs = measured_cell_position.shape[0]
    f32 = jnp.float32
    vmem = pl.BlockSpec(memory_space=pltpu.VMEM)
    hbm = pl.BlockSpec(memory_space=pltpu.HBM)
    dma = pltpu.SemaphoreType.DMA
    pieces = pltpu.VMEM((2 * n, 8, LANES), f32)
    fields, sums = pl.pallas_call(
        functools.partial(kernel, n, tiles, cols, obs, obs * tiles),
        out_shape=(
            pltpu.VMEM(state.shape, f32),
            pltpu.VMEM((2, 8, LANES), f32),
        ),
        in_specs=[hbm] * 6,
        out_specs=(vmem, vmem),
        scratch_shapes=[
            pltpu.SMEM((2 * n,), jnp.int32),
            pltpu.VMEM((1, obs), jnp.int32),
            pltpu.VMEM((1, obs), f32),
            pltpu.VMEM((1, obs), f32),
            pieces, pieces, pieces, pieces, pieces, pieces,
            pltpu.VMEM((2, 3, TALL, cols), f32),
            pltpu.VMEM((2, TALL, cols), f32),
            pltpu.VMEM((2, TALL, cols), f32),
            pltpu.VMEM((32, cols), f32),
            pltpu.VMEM((7 * 32, obs), jnp.bfloat16),
            pltpu.VMEM((3, TALL, cols), f32),
            pltpu.VMEM((2, tiles, 8, LANES), f32),
            dma((3,)), dma((3,)), dma((5,)), dma((4,)), dma((4,)),
            dma((4, 2)), dma((4, 2)), dma((2,)), dma((2,)),
        ],
        compiler_params=pltpu.CompilerParams(
            collective_id=0, has_side_effects=True, vmem_limit_bytes=32 * 1024 * 1024
        ),
    )(*(
        pltpu.with_memory_space_constraint(operand, pltpu.HBM)
        for operand in (
            parents,
            measured_cell_position.reshape(1, obs),
            obs_value.reshape(1, obs),
            obs_precision.reshape(1, obs),
            state,
            noise,
        )
    ))
    return pl.pallas_call(
        finish,
        out_shape=(jax.ShapeDtypeStruct(state.shape, f32), jax.ShapeDtypeStruct((2,), f32)),
        in_specs=[vmem, vmem],
        out_specs=(hbm, hbm),
        scratch_shapes=[pltpu.SMEM((2,), f32), dma((7,))],
    )(pltpu.with_memory_space_constraint(fields, pltpu.VMEM), pltpu.with_memory_space_constraint(sums, pltpu.VMEM))


def solution(mesh):
    placed = (
        P("dom", None, "tile", None),
        P("dom", "tile", None),
        P(),
        P("tile"),
        P("tile"),
        P("tile"),
    )
    return jax.shard_map(
        body,
        mesh=mesh,
        in_specs=placed,
        out_specs=(P("dom", None, "tile", None), P("dom")),
        check_vma=False,
    )
```

```python
import functools

import jax
import jax.numpy as jnp
from jax import lax
from jax.experimental import pallas as pl
from jax.experimental.pallas import tpu as pltpu
from jax.sharding import PartitionSpec as P

STEPS = 4
LANES = 128
HALO = 8
TALL = 48

COURANT = 1.2
CORIOLIS = 0.1
RELAXATION = 0.3

NOISE, GAIN, FIRST, SECOND = range(4)


def split_three(x):
    high = x.astype(jnp.bfloat16)
    rest = x - high.astype(jnp.float32)
    middle = rest.astype(jnp.bfloat16)
    low = (rest - middle.astype(jnp.float32)).astype(jnp.bfloat16)
    return high, middle, low


def kernel(
    n, tiles, cols, obs, obs_all,
    parents_in, position_in, value_in, precision_in, state, noise,
    result, mismatch_out,
    parents, position, value, precision,
    every0, every1, every2, pick0, pick1, pick2, fields, noise_all, nudge, weight, row_values, work, sums,
    spread_send, spread_recv, local_sem, back_send, back_recv, halo_send, halo_recv, sums_send, sums_recv,
):
    every = (every0, every1, every2)
    pick = (pick0, pick1, pick2)
    groups = cols // LANES
    dom = lax.axis_index("dom")
    tile = lax.axis_index("tile")
    has_above = tile > 0
    has_below = tile < tiles - 1

    def place(stage, j):
        column = pl.multiple_of((j % groups) * LANES, LANES)
        if stage == 0:
            field, row = j // (2 * groups), 3 * ((j // groups) % 2)
        elif stage == 1:
            field, row = 2, j // groups
        else:
            field, row = j // (2 * groups), 1 + (j // groups) % 2
        return field, row * 8, column

    def partner(i):
        planes = n // 4
        turn = i // 4
        away = (turn + 1) // 2
        ahead = jnp.where(turn % 2 == 1, away, planes - away)
        z = (dom // 4 + ahead) % planes
        return z * 4 + (dom % 4 + i % 4) % 4

    barrier = pltpu.get_barrier_semaphore()

    for i in range(n - 1, 0, -1):
        pl.semaphore_signal(barrier, 1, device_id={"dom": partner(i)})
    for i in range(1, tiles):
        pl.semaphore_signal(barrier, 1, device_id={"tile": (tile + i) % tiles})

    noise_copy = pltpu.make_async_copy(noise, noise_all.at[:, HALO:HALO + 32, :], local_sem.at[0])
    small_copies = [
        pltpu.make_async_copy(source, there, local_sem.at[1 + at])
        for at, (source, there) in enumerate(
            ((parents_in, parents), (position_in, position), (value_in, value), (precision_in, precision))
        )
    ]
    for copy in small_copies:
        copy.start()
    noise_copy.start()
    pl.semaphore_wait(barrier, n - 1 + tiles - 1)

    def spread(stage):
        def piece(j):
            field, row, column = place(stage, j)
            return state.at[:, field, pl.ds(pl.multiple_of(row, 8), 8), pl.ds(column, LANES)]

        mine = every[stage].at[pl.ds(2 * dom, 2)]

        @pl.loop(0, n)
        def _(i):
            target = (i // 4) * 4 + (dom + i) % 4

            @pl.when(target != dom)
            def _():
                pltpu.make_async_remote_copy(
                    piece(target), mine, spread_send.at[stage], spread_recv.at[stage], device_id={"dom": target}
                ).start()

        pltpu.make_async_copy(piece(dom), mine, spread_recv.at[stage]).start()

    def await_spread(stage):
        pltpu.make_async_copy(every[stage], every[stage], spread_recv.at[stage]).wait()

    def give_back(stage, first, count, sem):
        field, row, column = place(stage, dom)
        rows, lanes = pl.ds(pl.multiple_of(HALO + row, 8), 8), pl.ds(column, LANES)
        there = fields.at[pl.ds(first, count), field, rows, lanes]

        def choose(target):
            for p in range(first, first + count):
                pick[stage][2 * target + p] = every[stage][parents[2 * target + p]]

        @pl.loop(0, n)
        def _(i):
            target = (i // 4) * 4 + (dom + i) % 4
            choose(target)

            @pl.when(target != dom)
            def _():
                pltpu.make_async_remote_copy(
                    pick[stage].at[pl.ds(2 * target + first, count)], there,
                    back_send.at[sem], back_recv.at[sem], device_id={"dom": target},
                ).start()

        pltpu.make_async_copy(pick[stage].at[pl.ds(2 * dom + first, count)], there, back_recv.at[sem]).start()

    def await_back(sem, count):
        whole = pick[0].at[pl.ds(0, count * n)]
        pltpu.make_async_copy(whole, whole, back_recv.at[sem]).wait()

    def to_above(kind, source, there):
        return pltpu.make_async_remote_copy(
            source, there, halo_send.at[kind, 0], halo_recv.at[kind, 0], device_id={"tile": jnp.maximum(tile - 1, 0)}
        )

    def to_below(kind, source, there):
        return pltpu.make_async_remote_copy(
            source, there, halo_send.at[kind, 1], halo_recv.at[kind, 1],
            device_id={"tile": jnp.minimum(tile + 1, tiles - 1)},
        )

    top, bottom = pl.ds(HALO, HALO), pl.ds(HALO + 24, HALO)
    over, under = pl.ds(0, HALO), pl.ds(HALO + 32, HALO)

    def halos(kind):
        if kind == NOISE:
            up = to_above(kind, noise.at[:, pl.ds(0, HALO), :], noise_all.at[:, under, :])
            down = to_below(kind, noise.at[:, pl.ds(24, HALO), :], noise_all.at[:, over, :])
        elif kind == GAIN:
            up = to_above(kind, nudge.at[:, top, :], nudge.at[:, under, :])
            down = to_below(kind, nudge.at[:, bottom, :], nudge.at[:, over, :])
        else:
            which = pl.ds(0, 2) if kind == FIRST else pl.ds(2, 1)
            up = to_above(kind, fields.at[:, which, top, :], fields.at[:, which, under, :])
            down = to_below(kind, fields.at[:, which, bottom, :], fields.at[:, which, over, :])
        return up, down

    def send_halo(kind):
        up, down = halos(kind)

        @pl.when(has_above)
        def _():
            up.start()

        @pl.when(has_below)
        def _():
            down.start()

    def await_halo(kind):
        up, down = halos(kind)

        @pl.when(has_below)
        def _():
            up.wait_recv()

        @pl.when(has_above)
        def _():
            down.wait_recv()

    def await_halo_sent(kind):
        up, down = halos(kind)

        @pl.when(has_above)
        def _():
            up.wait_send()

        @pl.when(has_below)
        def _():
            down.wait_send()

    spread(0)
    spread(1)
    send_halo(NOISE)

    @pl.when(tile == 0)
    def _():
        fields[:, :, 0:HALO, :] = jnp.zeros((2, 3, HALO, cols), jnp.float32)
        noise_all[:, 0:HALO, :] = jnp.zeros((2, HALO, cols), jnp.float32)
        nudge[:, 0:HALO, :] = jnp.zeros((2, HALO, cols), jnp.float32)

    @pl.when(tile == tiles - 1)
    def _():
        fields[:, :, HALO + 32:, :] = jnp.zeros((2, 3, HALO, cols), jnp.float32)
        noise_all[:, HALO + 32:, :] = jnp.zeros((2, HALO, cols), jnp.float32)
        nudge[:, HALO + 32:, :] = jnp.zeros((2, HALO, cols), jnp.float32)

    for copy in small_copies:
        copy.wait()

    local = position[...] - tile * (32 * cols)
    row_of = local // cols
    column_of = local % cols
    in_row = lax.broadcasted_iota(jnp.int32, (32, obs), 0) == row_of

    def put(slot, row):
        spread_row = jnp.where(in_row, row.astype(jnp.float32), 0.0)
        row_values[slot * 32:(slot + 1) * 32, :] = spread_row.astype(jnp.bfloat16)

    put(0, jnp.ones((1, obs), jnp.float32))
    for at, part in enumerate(split_three(value[...])):
        put(1 + at, part)
    for at, part in enumerate(split_three(precision[...])):
        put(4 + at, part)

    wide = min(cols, 256)

    @pl.loop(0, cols // wide)
    def _(block):
        first = pl.multiple_of(block * wide, wide)
        column = lax.broadcasted_iota(jnp.int32, (wide, obs), 0) + first
        in_column = jnp.where(column == column_of, 1.0, 0.0).astype(jnp.bfloat16)
        grid = lax.dot_general(
            row_values[...], in_column, (((1,), (1,)), ((), ())), preferred_element_type=jnp.float32
        )
        lanes = pl.ds(first, wide)
        nudge[0, HALO:HALO + 32, lanes] = RELAXATION * grid[0:32]
        nudge[1, HALO:HALO + 32, lanes] = (grid[32:64] + grid[64:96]) + grid[96:128]
        weight[:, lanes] = (grid[128:160] + grid[160:192]) + grid[192:224]

    send_halo(GAIN)

    await_spread(0)
    give_back(0, 0, 2, 0)
    spread(2)
    await_spread(1)
    give_back(1, 0, 2, 1)
    await_back(0, 2)
    send_halo(FIRST)
    await_spread(2)
    give_back(2, 0, 1, 2)
    await_back(1, 2)
    send_halo(SECOND)
    give_back(2, 1, 1, 3)

    noise_copy.wait()
    for kind in range(4):
        await_halo(kind)

    row_id = lax.broadcasted_iota(jnp.int32, (TALL, cols), 0)
    inside = jnp.logical_and(
        jnp.logical_or(row_id >= HALO, has_above), jnp.logical_or(row_id < HALO + 32, has_below)
    )

    def column_change(a):
        return pltpu.roll(a, cols - 1, 1) - pltpu.roll(a, 1, 1)

    def row_change(a):
        return pltpu.roll(a, TALL - 1, 0) - pltpu.roll(a, 1, 0)

    half = 0.5 * COURANT

    def sums_copy(p, i):
        mine = sums.at[p, tile]
        return pltpu.make_async_remote_copy(
            mine, mine, sums_send.at[p], sums_recv.at[p], device_id={"tile": (tile + i) % tiles}
        )

    def forecast(p):
        for step in range(STEPS):
            if step == 0:
                h, u, v = fields[p, 0] + noise_all[p], fields[p, 1], fields[p, 2]
            else:
                h, u, v = work[0], work[1], work[2]
            h1 = h - half * (column_change(u) + row_change(v))
            h2 = h1 + nudge[0] * (nudge[1] - h1)
            if step == STEPS - 1:
                h2 = h2[HALO:HALO + 32]
                miss = nudge[1, HALO:HALO + 32, :] - h2
                miss = weight[...] * (miss * miss)
                total = jnp.zeros((8, LANES), jnp.float32)
                for r in range(4):
                    for c in range(groups):
                        total = total + miss[8 * r:8 * r + 8, LANES * c:LANES * (c + 1)]
                sums[p, tile] = total
                for i in sorted(range(1, tiles), key=lambda i: -min(i, tiles - i)):
                    sums_copy(p, i).start()
            u1 = u + CORIOLIS * v - half * column_change(h1)
            v1 = v - CORIOLIS * u - half * row_change(h1)
            if step < STEPS - 1:
                work[0] = jnp.where(inside, h2, 0.0)
                work[1] = jnp.where(inside, u1, 0.0)
                work[2] = jnp.where(inside, v1, 0.0)
            else:
                result[p, 0] = h2
                result[p, 1] = u1[HALO:HALO + 32]
                result[p, 2] = v1[HALO:HALO + 32]

    await_back(2, 1)
    forecast(0)
    await_back(3, 1)
    forecast(1)

    for p in range(2):
        others = sums.at[p, pl.ds(0, tiles - 1)]
        pltpu.make_async_copy(others, others, sums_recv.at[p]).wait()
        total = sums[p, 0]
        for t in range(1, tiles):
            total = total + sums[p, t]
        mismatch_out[p] = total * (0.5 / obs_all)

    for p in range(2):
        others = sums.at[p, pl.ds(0, tiles - 1)]
        pltpu.make_async_copy(others, others, sums_send.at[p]).wait()
    two = pick[0].at[pl.ds(0, 2 * (n - 1))]
    one = pick[0].at[pl.ds(0, n - 1)]
    for stage in range(3):
        pltpu.make_async_copy(two, two, spread_send.at[stage]).wait()
    for sem in range(4):
        sent = two if sem < 2 else one
        pltpu.make_async_copy(sent, sent, back_send.at[sem]).wait()
    for kind in range(4):
        await_halo_sent(kind)


def finish(fields, sums, fields_out, mismatch_out, both, sem):
    copies = [
        pltpu.make_async_copy(fields.at[p, f], fields_out.at[p, f], sem.at[3 * p + f]) for p in range(2) for f in range(3)
    ]
    for copy in copies:
        copy.start()
    for p in range(2):
        both[p] = jnp.sum(sums[p])
    copies.append(pltpu.make_async_copy(both, mismatch_out, sem.at[6]))
    copies[-1].start()
    for copy in copies:
        copy.wait()


def body(state, noise, parents, measured_cell_position, obs_value, obs_precision):
    n, tiles = lax.axis_size("dom"), lax.axis_size("tile")
    cols = state.shape[3]
    obs = measured_cell_position.shape[0]
    f32 = jnp.float32
    vmem = pl.BlockSpec(memory_space=pltpu.VMEM)
    hbm = pl.BlockSpec(memory_space=pltpu.HBM)
    dma = pltpu.SemaphoreType.DMA
    pieces = pltpu.VMEM((2 * n, 8, LANES), f32)
    fields, sums = pl.pallas_call(
        functools.partial(kernel, n, tiles, cols, obs, obs * tiles),
        out_shape=(
            pltpu.VMEM(state.shape, f32),
            pltpu.VMEM((2, 8, LANES), f32),
        ),
        in_specs=[hbm] * 6,
        out_specs=(vmem, vmem),
        scratch_shapes=[
            pltpu.SMEM((2 * n,), jnp.int32),
            pltpu.VMEM((1, obs), jnp.int32),
            pltpu.VMEM((1, obs), f32),
            pltpu.VMEM((1, obs), f32),
            pieces, pieces, pieces, pieces, pieces, pieces,
            pltpu.VMEM((2, 3, TALL, cols), f32),
            pltpu.VMEM((2, TALL, cols), f32),
            pltpu.VMEM((2, TALL, cols), f32),
            pltpu.VMEM((32, cols), f32),
            pltpu.VMEM((7 * 32, obs), jnp.bfloat16),
            pltpu.VMEM((3, TALL, cols), f32),
            pltpu.VMEM((2, tiles, 8, LANES), f32),
            dma((3,)), dma((3,)), dma((5,)), dma((4,)), dma((4,)),
            dma((4, 2)), dma((4, 2)), dma((2,)), dma((2,)),
        ],
        compiler_params=pltpu.CompilerParams(
            collective_id=0, has_side_effects=True, vmem_limit_bytes=32 * 1024 * 1024
        ),
    )(*(
        pltpu.with_memory_space_constraint(operand, pltpu.HBM)
        for operand in (
            parents,
            measured_cell_position.reshape(1, obs),
            obs_value.reshape(1, obs),
            obs_precision.reshape(1, obs),
            state,
            noise,
        )
    ))
    return pl.pallas_call(
        finish,
        out_shape=(jax.ShapeDtypeStruct(state.shape, f32), jax.ShapeDtypeStruct((2,), f32)),
        in_specs=[vmem, vmem],
        out_specs=(hbm, hbm),
        scratch_shapes=[pltpu.SMEM((2,), f32), dma((7,))],
    )(pltpu.with_memory_space_constraint(fields, pltpu.VMEM), pltpu.with_memory_space_constraint(sums, pltpu.VMEM))


def solution(mesh):
    placed = (
        P("dom", None, "tile", None),
        P("dom", "tile", None),
        P(),
        P("tile"),
        P("tile"),
        P("tile"),
    )
    return jax.shard_map(
        body,
        mesh=mesh,
        in_specs=placed,
        out_specs=(P("dom", None, "tile", None), P("dom")),
        check_vma=False,
    )
```
